256 devices in a mesh: users: 16 (over x_hi, z), seq: 16 (over x_lo, y, core).
Axes of the slice: x: 4 (x_hi: 2, x_lo: 2; x = x_hi * 2 + x_lo), y: 4, z: 8, core: 2. Of those that a mesh axis runs over, the one named last changes fastest.
Arguments:
- hist_qu: bfloat16 [16, 2048, 2, 512], P('users', 'seq'), may hold values from -6 to 6
- hist_kv: bfloat16 [16, 2048, 2, 512], P('users', 'seq'), may hold values from -6 to 6
- hist_x: bfloat16 [16, 2048, 1024], P('users', 'seq'), may hold values from -6 to 6
- lengths: int32 [16], P('users'), may hold values from 512 to 2048, as said below
- cand_qu: bfloat16 [16, 16, 384, 2, 512], P('users', 'seq'), may hold values from -6 to 6
- cand_owner: int32 [16, 16, 12], P('users', 'seq'), may hold values from 0 to 15, as said below
- w_out: bfloat16 [512, 1024], replicated, may hold values from -0.25 to 0.25
Outputs:
- hist_out: bfloat16 [16, 2048, 1024], P('users', 'seq')
- cand_out: bfloat16 [16, 16, 384, 1024], P('users', 'seq')
The draws below stay inside these ranges and needn't reach their ends.
Inputs may be any that keep to these rules, and one draw needn't show every extreme that they name: `lengths`: some user has exactly 2048 events. `cand_owner`: one device names one owner at most 2 times; for every index of seq some owner is named exactly 2 times by each device of that index.
All inputs are finite; a program needn't handle non-finite values.
Results may differ from the reference program's by a relative error of at most 0.0064.
Values may be sent and summed in bfloat16 or wider, within the bound.
A program may use at most 64 MiB of HBM per device.

```python
import math
import jax
import jax.numpy as jnp
from jax import lax

D = 1024
HEADS = 4
HEAD_DIM = 128
HD = 512
TILE = 32
TILES_DEV = 12
CAP = 2
USERS = 16
COLUMNS = 16
LENGTH = 2048
CROWS = 384


def draw_lengths(key, part):
    key = jax.random.fold_in(key, 11)
    first_key, second_key = jax.random.split(key)
    spread = jax.random.randint(first_key, (USERS,), LENGTH // 4, LENGTH + 1)
    longest = jax.random.randint(second_key, (), 0, USERS)
    return jnp.where(jnp.arange(USERS) == longest, LENGTH, spread).astype(jnp.int32)


def draw_cand_owner(key, part):
    key = jax.random.fold_in(key, 23)
    loaded_device_key, rest_key = jax.random.split(key)
    busiest = jax.random.randint(loaded_device_key, (COLUMNS,), 0, USERS).astype(jnp.int32)
    device_keys = jax.random.split(rest_key, USERS * COLUMNS)

    def one_device(device_key, favoured):
        other_key, order_key = jax.random.split(device_key)
        others = jax.random.permutation(other_key, USERS - 1).astype(jnp.int32)
        picks = jnp.arange(TILES_DEV - CAP, dtype=jnp.int32) % (USERS - 1)
        chosen = (favoured + 1 + others[picks]) % USERS
        owners = jnp.concatenate([jnp.full((CAP,), 1, jnp.int32) * favoured, chosen.astype(jnp.int32)])
        return owners[jax.random.permutation(order_key, TILES_DEV)]
    owners = jax.vmap(one_device)(device_keys, jnp.tile(busiest, USERS))
    return owners.reshape(USERS, COLUMNS, TILES_DEV).astype(jnp.int32)


def block_levels(stream_key, extent, pieces, smallest, top_value):
    factor_of, own = 1.0, jax.random.fold_in(stream_key, 6)
    for position, shards_of in pieces:
        draws = jnp.exp(jax.random.uniform(jax.random.fold_in(own, position), (shards_of,), jnp.float32, smallest / len(pieces), top_value / len(pieces)))
        factor_of = factor_of * jnp.repeat(draws, extent[position] // shards_of).reshape([-1 if axis == position else 1 for axis in range(len(extent))])
    return factor_of


def bell_draw(key, extent, scale, most, cuts=(), kind=jnp.bfloat16):
    loudness = block_levels(key, extent, cuts, -0.22, 0.18) if cuts else 1.0
    array = jax.random.normal(key, extent, jnp.float32) * scale * loudness
    return jnp.minimum(jnp.maximum(array, -most), most).astype(kind)


def setup_inputs(seed: int = 0) -> dict:
    splits = jax.random.split(jax.random.key(seed), 8)
    return {
        "hist_qu": bell_draw(splits[0], (USERS, LENGTH, 2, HD), 1.0, 6.0, ((0, 16), (1, 16))),
        "hist_kv": bell_draw(splits[1], (USERS, LENGTH, 2, HD), 1.0, 6.0, ((0, 16), (1, 16))),
        "hist_x": bell_draw(splits[2], (USERS, LENGTH, D), 1.0, 6.0, ((0, 16), (1, 16))),
        "lengths": draw_lengths(jax.random.fold_in(splits[7], 71), 0),
        "cand_qu": bell_draw(splits[4], (USERS, COLUMNS, CROWS, 2, HD), 1.0, 6.0, ((0, 16), (1, 16))),
        "cand_owner": draw_cand_owner(jax.random.fold_in(splits[7], 71), 0),
        "w_out": bell_draw(splits[6], (HD, D), HD ** -0.5, 0.25),
    }


EPS = 1e-05

def pointwise_silu_weight(queries, keys, qpos, kpos, limit):
    scores = jnp.einsum('qhd,khd->hqk', queries.astype(jnp.float32), keys.astype(jnp.float32)) * (1.0 / math.sqrt(HEAD_DIM))
    allowed = (kpos[None, :] < limit) & (kpos[None, :] <= qpos[:, None])
    return jnp.where(allowed[None], jax.nn.silu(scores), 0.0).astype(jnp.bfloat16)

def gate_rows(summed, gates):
    mean = lax.optimization_barrier(jnp.mean(summed, axis=-1, keepdims=True))
    centred = summed - mean
    spread = lax.optimization_barrier(jnp.mean(centred * centred, axis=-1, keepdims=True))
    normed = lax.optimization_barrier((centred * lax.rsqrt(spread + EPS)).astype(jnp.bfloat16))
    return (normed.astype(jnp.float32) * gates.astype(jnp.float32)).astype(jnp.bfloat16)

def reference(hist_qu, hist_kv, hist_x, lengths, cand_qu, cand_owner, w_out):
    block = min(512, LENGTH)
    token_positions = jnp.arange(LENGTH, dtype=jnp.int32)

    def one_user(items):
        rows_qu, rows_kv, input_rows_matrix, limit = items
        keys = rows_kv[:, 0].reshape(LENGTH, HEADS, HEAD_DIM)
        value_rows = rows_kv[:, 1].reshape(LENGTH, HEADS, HEAD_DIM)

        def one_block(index):
            first = index * block
            queries = lax.dynamic_slice_in_dim(rows_qu[:, 0], first, block, 0).reshape(block, HEADS, HEAD_DIM)
            gates = lax.dynamic_slice_in_dim(rows_qu[:, 1], first, block, 0)
            inputs = lax.dynamic_slice_in_dim(input_rows_matrix, first, block, 0)
            qpos = first + jnp.arange(block, dtype=jnp.int32)
            weights = pointwise_silu_weight(queries, keys, qpos, token_positions, limit)
            summed = jnp.einsum('hqk,khd->qhd', weights.astype(jnp.float32), value_rows.astype(jnp.float32)).reshape(block, HD)
            gated = gate_rows(summed, gates)
            result = jnp.dot(gated, w_out, preferred_element_type=jnp.float32) + inputs.astype(jnp.float32)
            return jnp.where((qpos < limit)[:, None], result, 0.0).astype(jnp.bfloat16)
        blocks = lax.map(one_block, jnp.arange(LENGTH // block, dtype=jnp.int32))
        return blocks.reshape(LENGTH, D)
    hist_out = lax.map(one_user, (hist_qu, hist_kv, hist_x, lengths))
    flat_qu = cand_qu.reshape(USERS * COLUMNS, TILES_DEV, TILE, 2, HD)
    flat_owner = cand_owner.reshape(USERS * COLUMNS, TILES_DEV)

    def one_device(items):
        tiles, owners = items
        keys = hist_kv[owners, :, 0].reshape(TILES_DEV, LENGTH, HEADS, HEAD_DIM)
        value_rows = hist_kv[owners, :, 1].reshape(TILES_DEV, LENGTH, HEADS, HEAD_DIM)
        limits = lengths[owners]
        queries = tiles[:, :, 0].reshape(TILES_DEV, TILE, HEADS, HEAD_DIM)
        scores = jnp.einsum('trhd,tkhd->thrk', queries.astype(jnp.float32), keys.astype(jnp.float32)) * (1.0 / math.sqrt(HEAD_DIM))
        allowed = token_positions[None, :] < limits[:, None]
        weights = jnp.where(allowed[:, None, None, :], jax.nn.silu(scores), 0.0).astype(jnp.bfloat16)
        summed = jnp.einsum('thrk,tkhd->trhd', weights.astype(jnp.float32), value_rows.astype(jnp.float32)).reshape(TILES_DEV * TILE, HD)
        gated = gate_rows(summed, tiles[:, :, 1].reshape(TILES_DEV * TILE, HD))
        return jnp.dot(gated, w_out, preferred_element_type=jnp.float32).astype(jnp.bfloat16)
    cand_out = lax.map(one_device, (flat_qu, flat_owner)).reshape(USERS, COLUMNS, CROWS, D)
    return (hist_out, cand_out)
```

```python
import functools
import math

import jax
import jax.numpy as jnp
from jax import lax
from jax.experimental import pallas as pl
from jax.experimental.pallas import tpu as pltpu
from jax.sharding import PartitionSpec as P

HEADS = 4
HEAD_DIM = 128
WIDTH = HEADS * HEAD_DIM
CAP = 2
TILE = 32
TILES = 12
CROWS = TILES * TILE
ROWS = 128
LENGTH = 2048
MODEL = 1024
EPS = 1e-05
HALF_SCALE = 0.5 / math.sqrt(HEAD_DIM)

ZS, YS = 8, 4
HOPS = 4
MESSAGES = HOPS * 4
PACK = CAP * TILE
BATCH = 512
BATCHES = MESSAGES * PACK // BATCH
PER_BATCH = MESSAGES // BATCHES


def _mod(value, size):
    return lax.rem(value + 2 * size, size)


def _user(x_hi, z):
    return _mod(x_hi, 2) * ZS + _mod(z, ZS)


def _seq(x_lo, y, core):
    return _mod(x_lo, 2) * (YS * 2) + _mod(y, YS) * 2 + _mod(core, 2)


def _send(src, dst, send_sem, recv_sem, device):
    return pltpu.make_async_remote_copy(
        src_ref=src,
        dst_ref=dst,
        send_sem=send_sem,
        recv_sem=recv_sem,
        device_id=device,
        device_id_type=pl.DeviceIdType.MESH,
    )


def _silu_weights(scores):
    half = scores * HALF_SCALE
    return half + half * jnp.tanh(half)


def _normalise(summed):
    mean = jnp.mean(summed, axis=-1, keepdims=True)
    centred = summed - mean
    spread = jnp.mean(centred * centred, axis=-1, keepdims=True)
    return (centred * lax.rsqrt(spread + EPS)).astype(jnp.bfloat16)


def _every_second(rows, first):
    count = rows.shape[0] // 2
    at = 2 * lax.broadcasted_iota(jnp.int32, (count, 2 * count), 0) + first
    column = lax.broadcasted_iota(jnp.int32, (count, 2 * count), 1)
    return jnp.dot(
        jnp.where(column == at, 1.0, 0.0).astype(jnp.bfloat16),
        rows,
        preferred_element_type=jnp.float32,
    ).astype(jnp.bfloat16)


def _gate(normed, gates):
    return (normed.astype(jnp.float32) * gates.astype(jnp.float32)).astype(jnp.bfloat16)


def kernel(
    qu_ref, kv_ref, x_ref, lengths_ref, cand_ref, owner_ref, w_ref,
    hist_out, cand_out,
    own_kv, kv, hist_q, hist_part, hist_done, cand_rows, cand_g, hist_g, outgoing, arrived, computed,
    returned, acc, pick,
    kv_send, kv_recv, q_send, q_recv, r_send, r_recv, h_send, h_recv,
):
    user = lax.axis_index("users")
    seq = lax.axis_index("seq")
    x_hi, z = user // ZS, user % ZS
    x_lo, y, core = seq // (YS * 2), (seq // 2) % YS, seq % 2
    home_x = z // 4
    native = x_lo == home_x

    far = jnp.where(core == 0, 2, -2)
    steps = (0, 1, far, -1)

    def peer(m, back):
        step, a, b = steps[m // 4], (m // 2) % 2, m % 2
        other_z = z + step if back else z - step
        return (_user(x_hi + a, other_z), _seq(x_lo + b, y, core))

    partner = (user, _seq(x_lo, y, core + 1))
    y_up = (user, _seq(x_lo, y + 1, core))
    y_down = (user, _seq(x_lo, y - 1, core))
    x_other = (user, _seq(x_lo + 1, y, core))
    opposite = _user(x_hi, z + 4)

    barrier = pltpu.get_barrier_semaphore()
    greeted = [partner, y_up, y_down]
    greeted += [(opposite, _seq(x_lo, y, core)), (opposite, _seq(x_lo + 1, y, core))]
    greeted += [peer(m, False) for m in range(1, MESSAGES)]
    greeted += [peer(m, True) for m in range(8, 12)]
    for device in greeted:
        pl.semaphore_signal(
            barrier, inc=1, device_id=device, device_id_type=pl.DeviceIdType.MESH
        )

    limit = lengths_ref[0]
    position = seq * ROWS + lax.broadcasted_iota(jnp.int32, (ROWS, WIDTH), 0)
    rows_kv = kv_ref[0].reshape(2 * ROWS, WIDTH)
    own_kv[0] = _every_second(rows_kv, 0)
    own_kv[1] = jnp.where(position < limit, _every_second(rows_kv, 1), jnp.zeros((), jnp.bfloat16))
    hist_q[0] = _every_second(qu_ref[0].reshape(2 * ROWS, WIDTH), 0)

    pl.semaphore_wait(barrier, len(greeted))

    def shard(index):
        return kv.at[:, pl.ds(pl.multiple_of(index * ROWS, ROWS), ROWS), :]

    to_far = _send(
        own_kv, shard(seq), kv_send.at[0], kv_recv.at[seq], (opposite, _seq(home_x, y, core))
    )
    to_near = _send(own_kv, shard(seq), kv_send.at[1], kv_recv.at[seq], x_other)
    q_over = _send(hist_q.at[0], hist_q.at[1], h_send.at[0], h_recv.at[0], x_other)
    to_far.start()

    @pl.when(jnp.logical_not(native))
    def _():
        to_near.start()
        q_over.start()

    @pl.when(native)
    def _():
        kv[:, pl.ds(pl.multiple_of(seq * ROWS, ROWS), ROWS), :] = own_kv[...]

    owners = [owner_ref[0, 0, t] for t in range(TILES)]

    def slot_rows(index):
        tile = index // TILE
        owner = jnp.zeros_like(index)
        for t in range(TILES):
            owner = jnp.where(tile == t, owners[t], owner)
        again = jnp.zeros_like(index)
        for t in range(TILES - 1):
            again = jnp.where((tile > t) & (owner == owners[t]), 1, again)
        owner_x, owner_z = owner >> 3, owner & 7
        a, b = (owner_x + x_hi) & 1, ((owner_z >> 2) + x_lo) & 1
        message = ((z + 8 - owner_z) & 3) * 4 + a * 2 + b
        return message * PACK + again * TILE + (index & (TILE - 1))

    for t in range(TILES * TILE // ROWS):
        cand_rows[pl.ds(t * 2 * ROWS, 2 * ROWS), :] = cand_ref[
            0, 0, t * ROWS : (t + 1) * ROWS
        ].reshape(2 * ROWS, WIDTH)
    column = lax.broadcasted_iota(jnp.int32, (8, 2 * CROWS), 1)
    slot = jnp.where((column & 1) == 0, slot_rows(column >> 1), -1)[:1]
    q_copies = [None] * MESSAGES
    for step in (2, 1, 3, 0):
        block = pl.ds(step * 4 * PACK, 4 * PACK)
        row = step * 4 * PACK + lax.broadcasted_iota(jnp.int32, (4 * PACK, 2 * CROWS), 0)
        outgoing[block, :] = jnp.dot(
            jnp.where(row == slot, 1.0, 0.0).astype(jnp.bfloat16),
            cand_rows[...],
            preferred_element_type=jnp.float32,
        ).astype(jnp.bfloat16)
        for m in range(step * 4, step * 4 + 4):
            part = pl.ds(m * PACK, PACK)
            if m:
                q_copies[m] = _send(
                    outgoing.at[part], arrived.at[part], q_send.at[m], q_recv.at[m], peer(m, False)
                )
                q_copies[m].start()
            else:
                arrived[part, :] = outgoing[part, :]

    kv_copies = []

    def forward(index, device):
        copy = _send(
            shard(index), shard(index), kv_send.at[2 + len(kv_copies)], kv_recv.at[index], device
        )
        copy.start()
        kv_copies.append(copy)

    def await_shard(index):
        _send(shard(index), shard(index), kv_send.at[0], kv_recv.at[index], partner).wait_recv()

    for side in range(2):
        index = _seq(side, y, core)

        @pl.when(jnp.logical_not(jnp.logical_and(native, x_lo == side)))
        def _():
            await_shard(index)

        forward(index, y_up)
        forward(index, y_down)
        forward(index, partner)

    for t in range(TILES * TILE // ROWS):
        cand_g[pl.ds(t * ROWS, ROWS), :] = _every_second(
            cand_rows[pl.ds(t * 2 * ROWS, 2 * ROWS), :], 1
        )
    hist_g[...] = _every_second(qu_ref[0].reshape(2 * ROWS, WIDTH), 1)
    for t in range(TILES * TILE // ROWS):
        held = slot_rows(t * ROWS + lax.broadcasted_iota(jnp.int32, (ROWS, 128), 0))
        at = lax.broadcasted_iota(jnp.int32, (ROWS, MESSAGES * PACK), 1)
        pick[pl.ds(t * ROWS, ROWS), :] = jnp.where(at == held[:, :1], 1.0, 0.0).astype(jnp.bfloat16)

    for side, dy, onward in (
        (0, -1, y_up), (1, 1, y_down), (1, -1, None), (0, 1, None), (0, 2, None), (1, 2, None),
    ):
        index = _seq(side, y + dy, core)
        await_shard(index)
        if onward is not None:
            forward(index, onward)
        forward(index, partner)
    for side in range(2):
        for dy in range(YS):
            await_shard(_seq(side, y + dy, core + 1))

    def attend(queries, count, allowed=None):
        for h in range(HEADS):
            part = slice(h * HEAD_DIM, (h + 1) * HEAD_DIM)
            scores = lax.dot_general(
                queries[:, part],
                kv[0, :, part],
                (((1,), (1,)), ((), ())),
                preferred_element_type=jnp.float32,
            )
            weights = _silu_weights(scores)
            if allowed is not None:
                weights = jnp.where(allowed, weights, 0.0)
            acc[pl.ds(0, count), part] = jnp.dot(
                weights.astype(jnp.bfloat16),
                kv[1, :, part],
                preferred_element_type=jnp.float32,
            )
        return _normalise(acc[pl.ds(0, count), :])

    back_over = _send(hist_part, hist_done, h_send.at[1], h_recv.at[1], x_other)

    @pl.when(native)
    def _():
        q_over.wait_recv()
        key_at = lax.broadcasted_iota(jnp.int32, (ROWS, LENGTH), 1)
        row_at = lax.broadcasted_iota(jnp.int32, (ROWS, LENGTH), 0)
        other = _seq(x_lo + 1, y, core)
        hist_part[...] = attend(hist_q[1], ROWS, key_at <= row_at + other * ROWS)
        back_over.start()
        hist_done[...] = attend(hist_q[0], ROWS, key_at <= row_at + seq * ROWS)

    r_copies = []
    for batch in range(BATCHES):
        for m in range(batch * PER_BATCH, (batch + 1) * PER_BATCH):
            if m:
                q_copies[m].wait_recv()
        part = pl.ds(batch * BATCH, BATCH)
        computed[part, :] = attend(arrived[part, :], BATCH)
        for m in range(batch * PER_BATCH, (batch + 1) * PER_BATCH):
            part = pl.ds(m * PACK, PACK)
            if m:
                copy = _send(
                    computed.at[part], returned.at[part], r_send.at[m], r_recv.at[m], peer(m, True)
                )
                copy.start()
                r_copies.append(copy)
            else:
                returned[part, :] = computed[part, :]

    @pl.when(jnp.logical_not(native))
    def _():
        back_over.wait_recv()

    hist_rows = jnp.dot(
        _gate(hist_done[...], hist_g[...]), w_ref[...], preferred_element_type=jnp.float32
    ) + x_ref[0].astype(jnp.float32)
    row = seq * ROWS + lax.broadcasted_iota(jnp.int32, (ROWS, MODEL), 0)
    hist_out[0] = jnp.where(row < limit, hist_rows, 0.0).astype(jnp.bfloat16)

    for copy in r_copies:
        copy.wait_recv()
    picked = jnp.dot(pick[...], returned[...], preferred_element_type=jnp.float32)
    cand_out[0, 0] = jnp.dot(
        _gate(picked, cand_g[...]), w_ref[...], preferred_element_type=jnp.float32
    ).astype(jnp.bfloat16)

    to_far.wait_send()

    @pl.when(jnp.logical_not(native))
    def _():
        to_near.wait_send()
        q_over.wait_send()

    @pl.when(native)
    def _():
        back_over.wait_send()

    for copy in kv_copies + q_copies[1:] + r_copies:
        copy.wait_send()


def local(hist_qu, hist_kv, hist_x, lengths, cand_qu, cand_owner, w_out):
    vmem = pl.BlockSpec(memory_space=pltpu.VMEM)
    smem = pl.BlockSpec(memory_space=pltpu.SMEM)
    bf16 = jnp.bfloat16
    return pl.pallas_call(
        kernel,
        out_shape=(
            jax.ShapeDtypeStruct((1, ROWS, MODEL), bf16),
            jax.ShapeDtypeStruct((1, 1, CROWS, MODEL), bf16),
        ),
        in_specs=[vmem, vmem, vmem, smem, vmem, smem, vmem],
        out_specs=(vmem, vmem),
        scratch_shapes=[
            pltpu.VMEM((2, ROWS, WIDTH), bf16),
            pltpu.VMEM((2, LENGTH, WIDTH), bf16),
            pltpu.VMEM((2, ROWS, WIDTH), bf16),
            pltpu.VMEM((ROWS, WIDTH), bf16),
            pltpu.VMEM((ROWS, WIDTH), bf16),
            pltpu.VMEM((2 * CROWS, WIDTH), bf16),
            pltpu.VMEM((CROWS, WIDTH), bf16),
            pltpu.VMEM((ROWS, WIDTH), bf16),
            pltpu.VMEM((MESSAGES * PACK, WIDTH), bf16),
            pltpu.VMEM((MESSAGES * PACK, WIDTH), bf16),
            pltpu.VMEM((MESSAGES * PACK, WIDTH), bf16),
            pltpu.VMEM((MESSAGES * PACK, WIDTH), bf16),
            pltpu.VMEM((BATCH, WIDTH), jnp.float32),
            pltpu.VMEM((CROWS, MESSAGES * PACK), bf16),
            pltpu.SemaphoreType.DMA((16,)),
            pltpu.SemaphoreType.DMA((16,)),
            pltpu.SemaphoreType.DMA((MESSAGES,)),
            pltpu.SemaphoreType.DMA((MESSAGES,)),
            pltpu.SemaphoreType.DMA((MESSAGES,)),
            pltpu.SemaphoreType.DMA((MESSAGES,)),
            pltpu.SemaphoreType.DMA((2,)),
            pltpu.SemaphoreType.DMA((2,)),
        ],
        compiler_params=pltpu.CompilerParams(
            collective_id=0, has_side_effects=True, vmem_limit_bytes=50 * 2**20
        ),
    )(hist_qu, hist_kv, hist_x, lengths, cand_qu, cand_owner, w_out)


def solution(mesh):
    placed = (
        P("users", "seq", None, None),
        P("users", "seq", None, None),
        P("users", "seq", None),
        P("users"),
        P("users", "seq", None, None, None),
        P("users", "seq", None),
        P(),
    )
    return jax.shard_map(
        local,
        mesh=mesh,
        in_specs=placed,
        out_specs=(P("users", "seq", None), P("users", "seq", None, None)),
        check_vma=False,
    )
```

```python
import functools
import math

import jax
import jax.numpy as jnp
from jax import lax
from jax.experimental import pallas as pl
from jax.experimental.pallas import tpu as pltpu
from jax.sharding import PartitionSpec as P

HEADS = 4
HEAD_DIM = 128
WIDTH = HEADS * HEAD_DIM
CAP = 2
TILE = 32
TILES = 12
CROWS = TILES * TILE
ROWS = 128
LENGTH = 2048
MODEL = 1024
EPS = 1e-05
HALF_SCALE = 0.5 / math.sqrt(HEAD_DIM)

ZS, YS = 8, 4
STEPS = 4
MESSAGES = STEPS * 4
Q_ORDER = (12, 13, 14, 15, 4, 8, 5, 9, 6, 10, 7, 11, 1, 2, 3)
PACK = CAP * TILE
PACKED = MESSAGES * PACK
GROUPS = ((0, 8), (8, 8))
QUERY_HEADS = 1
BACK_HEADS = 1


def _mod(value, size):
    return lax.rem(value + 2 * size, size)


def _user(x_hi, z):
    return _mod(x_hi, 2) * ZS + _mod(z, ZS)


def _seq(x_lo, y, core):
    return _mod(x_lo, 2) * (YS * 2) + _mod(y, YS) * 2 + _mod(core, 2)


def _send(src, dst, send_sem, recv_sem, device):
    return pltpu.make_async_remote_copy(
        src_ref=src,
        dst_ref=dst,
        send_sem=send_sem,
        recv_sem=recv_sem,
        device_id=device,
        device_id_type=pl.DeviceIdType.MESH,
    )


def _silu_weights(scores):
    half = scores * HALF_SCALE
    return half + half * jnp.tanh(half)


def _normalise(summed):
    mean = jnp.mean(summed, axis=-1, keepdims=True)
    centred = summed - mean
    spread = jnp.mean(centred * centred, axis=-1, keepdims=True)
    return (centred * lax.rsqrt(spread + EPS)).astype(jnp.bfloat16)


def _every_second(rows, first):
    count = rows.shape[0] // 2
    at = 2 * lax.broadcasted_iota(jnp.int32, (count, 2 * count), 0) + first
    column = lax.broadcasted_iota(jnp.int32, (count, 2 * count), 1)
    return jnp.dot(
        jnp.where(column == at, 1.0, 0.0).astype(jnp.bfloat16),
        rows,
        preferred_element_type=jnp.float32,
    ).astype(jnp.bfloat16)


def _gate(normed, gates):
    return (normed.astype(jnp.float32) * gates.astype(jnp.float32)).astype(jnp.bfloat16)


def kernel(
    qu_hbm, kv_hbm, x_hbm, lengths_hbm, cand_hbm, owner_hbm, w_hbm,
    hist_out, cand_out,
    qu_ref, kv_ref, x_ref, lengths_ref, cand_ref, owner_ref, w_ref,
    own_kv, kv, hist_q, hist_done, cand_rows, cand_g, hist_g, outgoing, arrived, computed,
    returned, pick,
    loaded, kv_send, kv_recv, q_send, q_recv, r_send, r_recv, h_send, h_recv,
):
    user = lax.axis_index("users")
    seq = lax.axis_index("seq")
    x_hi, z = user // ZS, user % ZS
    x_lo, y, core = seq // (YS * 2), (seq // 2) % YS, seq % 2
    home_x = z % 2
    native = x_lo == home_x
    up = 1 - 2 * home_x
    steps = (0, 1, -1, 2)

    def peer(m, back):
        step, a, b = steps[m // 4], (m // 2) % 2, m % 2
        along = -2 if back and step == 2 else step
        return (_user(x_hi + a, z + up * along), _seq(x_lo + b, y, core))

    partner = (user, _seq(x_lo, y, core + 1))
    y_up = (user, _seq(x_lo, y + 1, core))
    y_down = (user, _seq(x_lo, y - 1, core))
    x_other = (user, _seq(x_lo + 1, y, core))
    mate = _user(x_hi, z + 3 * up)

    barrier = pltpu.get_barrier_semaphore()
    greeted = [partner, y_up, y_down]
    greeted += [(mate, _seq(x_lo, y, core)), (mate, _seq(x_lo + 1, y, core))]
    greeted += [peer(m, False) for m in range(1, MESSAGES)]
    greeted += [peer(m, True) for m in range(12, 16)]
    for device in greeted:
        pl.semaphore_signal(
            barrier, inc=1, device_id=device, device_id_type=pl.DeviceIdType.MESH
        )

    pairs = (
        (kv_hbm, kv_ref), (lengths_hbm, lengths_ref), (qu_hbm, qu_ref), (cand_hbm, cand_ref),
        (owner_hbm, owner_ref), (w_hbm, w_ref), (x_hbm, x_ref),
    )
    loads = [pltpu.make_async_copy(a, b, loaded.at[i]) for i, (a, b) in enumerate(pairs)]
    for load in loads:
        load.start()

    loads[0].wait()
    loads[1].wait()
    limit = lengths_ref[0]
    position = seq * ROWS + lax.broadcasted_iota(jnp.int32, (ROWS, WIDTH), 0)
    rows_kv = kv_ref[0].reshape(2 * ROWS, WIDTH)
    keys = _every_second(rows_kv, 0)
    values = jnp.where(position < limit, _every_second(rows_kv, 1), jnp.zeros((), jnp.bfloat16))
    for h in range(HEADS):
        part = slice(h * HEAD_DIM, (h + 1) * HEAD_DIM)
        own_kv[h, 0] = keys[:, part]
        own_kv[h, 1] = values[:, part]
    loads[2].wait()
    hist_q[:ROWS, :] = _every_second(qu_ref[0].reshape(2 * ROWS, WIDTH), 0)

    pl.semaphore_wait(barrier, len(greeted))

    def shard(h, index):
        return kv.at[h, :, pl.ds(pl.multiple_of(index * ROWS, ROWS), ROWS), :]

    home = _seq(home_x, y, core)
    to_far = [
        _send(
            own_kv.at[h], shard(h, seq), kv_send.at[h], kv_recv.at[seq, h], (mate, home)
        )
        for h in range(HEADS)
    ]
    to_near = [
        _send(own_kv.at[h], shard(h, seq), kv_send.at[4 + h], kv_recv.at[seq, h], x_other)
        for h in range(HEADS)
    ]
    q_over = _send(
        hist_q.at[pl.ds(0, ROWS)], hist_q.at[pl.ds(ROWS, ROWS)], h_send.at[0], h_recv.at[0], x_other
    )
    for copy in to_far:
        copy.start()

    @pl.when(jnp.logical_not(native))
    def _():
        for copy in to_near:
            copy.start()
        q_over.start()

    @pl.when(native)
    def _():
        kv[:, :, pl.ds(pl.multiple_of(seq * ROWS, ROWS), ROWS), :] = own_kv[...]

    loads[3].wait()
    loads[4].wait()
    owners = [owner_ref[0, 0, t] for t in range(TILES)]

    def slot_rows(index):
        tile = index // TILE
        owner = jnp.zeros_like(index)
        for t in range(TILES):
            owner = jnp.where(tile == t, owners[t], owner)
        again = jnp.zeros_like(index)
        for t in range(TILES - 1):
            again = jnp.where((tile > t) & (owner == owners[t]), 1, again)
        owner_x, owner_z = owner >> 3, owner & 7
        a, b = (owner_x + x_hi) & 1, (owner_z + x_lo) & 1
        apart = (up * (owner_z - z)) & 7
        step = jnp.zeros_like(index)
        for there in ((1, 6), (4, 7), (2, 5)):
            here = (apart == there[0]) | (apart == there[1])
            step = jnp.where(here, 1 + ((1, 6), (4, 7), (2, 5)).index(there), step)
        message = step * 4 + a * 2 + b
        return message * PACK + again * TILE + (index & (TILE - 1))

    for t in range(TILES * TILE // ROWS):
        cand_rows[pl.ds(t * 2 * ROWS, 2 * ROWS), :] = cand_ref[
            0, 0, t * ROWS : (t + 1) * ROWS
        ].reshape(2 * ROWS, WIDTH)
    column = lax.broadcasted_iota(jnp.int32, (8, 2 * CROWS), 1)
    slot = jnp.where((column & 1) == 0, slot_rows(column >> 1), -1)[:1]
    for step in range(STEPS):
        block = pl.ds(step * 4 * PACK, 4 * PACK)
        row = step * 4 * PACK + lax.broadcasted_iota(jnp.int32, (4 * PACK, 2 * CROWS), 0)
        outgoing[block, :] = jnp.dot(
            jnp.where(row == slot, 1.0, 0.0).astype(jnp.bfloat16),
            cand_rows[...],
            preferred_element_type=jnp.float32,
        ).astype(jnp.bfloat16)
    own_rows = pl.ds(0, PACK)
    arrived[own_rows, :] = outgoing[own_rows, :]

    def columns(first, count):
        return pl.ds(first * HEAD_DIM, count * HEAD_DIM)

    q_copies = {}
    for h in range(0, HEADS, QUERY_HEADS):
        for m in Q_ORDER:
            part = (pl.ds(m * PACK, PACK), columns(h, QUERY_HEADS))
            q_copies[m, h] = _send(
                outgoing.at[part], arrived.at[part], q_send.at[m, h], q_recv.at[m, h], peer(m, False)
            )
            q_copies[m, h].start()

    kv_copies = []

    def forward(h, index, device):
        copy = _send(
            shard(h, index),
            shard(h, index),
            kv_send.at[8 + len(kv_copies)],
            kv_recv.at[index, h],
            device,
        )
        copy.start()
        kv_copies.append(copy)

    def await_shard(h, index):
        _send(
            shard(h, index), shard(h, index), kv_send.at[0], kv_recv.at[index, h], partner
        ).wait_recv()

    def enter(h):
        for side in range(2):
            index = _seq(side, y, core)

            @pl.when(jnp.logical_not(jnp.logical_and(native, x_lo == side)))
            def _():
                await_shard(h, index)

            forward(h, index, y_up)
            forward(h, index, y_down)
            forward(h, index, partner)

    def first_hop(h):
        for side, dy, onward in ((0, -1, y_up), (1, 1, y_down), (1, -1, None), (0, 1, None)):
            index = _seq(side, y + dy, core)
            await_shard(h, index)
            if onward is not None:
                forward(h, index, onward)
            forward(h, index, partner)

    def second_hop(h):
        for side in range(2):
            index = _seq(side, y + 2, core)
            await_shard(h, index)
            forward(h, index, partner)

    def other_core(h):
        for side in range(2):
            for dy in range(YS):
                await_shard(h, _seq(side, y + dy, core + 1))

    def attend(h, queries, allowed=None):
        scores = lax.dot_general(
            queries, kv[h, 0], (((1,), (1,)), ((), ())), preferred_element_type=jnp.float32
        )
        weights = _silu_weights(scores)
        if allowed is not None:
            weights = jnp.where(allowed, weights, 0.0)
        return jnp.dot(
            weights.astype(jnp.bfloat16), kv[h, 1], preferred_element_type=jnp.float32
        )

    def prepare():
        for t in range(TILES * TILE // ROWS):
            cand_g[pl.ds(t * ROWS, ROWS), :] = _every_second(
                cand_rows[pl.ds(t * 2 * ROWS, 2 * ROWS), :], 1
            )
        hist_g[...] = _every_second(qu_ref[0].reshape(2 * ROWS, WIDTH), 1)
        for t in range(TILES * TILE // ROWS):
            held = slot_rows(t * ROWS + lax.broadcasted_iota(jnp.int32, (ROWS, 128), 0))
            at = lax.broadcasted_iota(jnp.int32, (ROWS, PACKED), 1)
            pick[pl.ds(t * ROWS, ROWS), :] = jnp.where(at == held[:, :1], 1.0, 0.0).astype(jnp.bfloat16)

    r_copies = []

    def group(h, g):
        first, count = GROUPS[g]
        if h % QUERY_HEADS == 0:
            for m in range(max(first, 1), first + count):
                q_copies[m, h].wait_recv()
        rows = pl.ds(first * PACK, count * PACK)
        part = columns(h, 1)
        computed[rows, part] = attend(h, arrived[rows, part]).astype(jnp.bfloat16)
        if (h + 1) % BACK_HEADS:
            return
        start = h + 1 - BACK_HEADS
        for m in range(first, first + count):
            part = (pl.ds(m * PACK, PACK), columns(start, BACK_HEADS))
            if m:
                copy = _send(
                    computed.at[part],
                    returned.at[part],
                    r_send.at[m, start],
                    r_recv.at[m, start],
                    peer(m, True),
                )
                copy.start()
                r_copies.append(copy)
            else:
                returned[part] = computed[part]

    enter(0)
    enter(1)
    first_hop(0)
    prepare()
    enter(2)
    first_hop(1)
    second_hop(0)
    enter(3)
    other_core(0)
    first_hop(2)
    second_hop(1)
    first_hop(3)
    second_hop(2)
    group(0, 0)
    other_core(1)
    second_hop(3)
    group(0, 1)
    group(1, 0)
    other_core(2)
    group(1, 1)
    group(2, 0)
    other_core(3)
    group(2, 1)
    group(3, 0)
    group(3, 1)

    back_over = _send(
        hist_done.at[pl.ds(ROWS, ROWS)],
        hist_done.at[pl.ds(0, ROWS)],
        h_send.at[1],
        h_recv.at[1],
        x_other,
    )

    @pl.when(native)
    def _():
        q_over.wait_recv()
        other = _seq(x_lo + 1, y, core)
        key_at = lax.broadcasted_iota(jnp.int32, (2 * ROWS, LENGTH), 1)
        row_at = lax.broadcasted_iota(jnp.int32, (2 * ROWS, LENGTH), 0)
        row_at = row_at + jnp.where(row_at < ROWS, seq * ROWS, (other - 1) * ROWS)
        for h in range(HEADS):
            part = slice(h * HEAD_DIM, (h + 1) * HEAD_DIM)
            hist_done[:, part] = attend(h, hist_q[:, part], key_at <= row_at).astype(jnp.bfloat16)
        back_over.start()

    @pl.when(jnp.logical_not(native))
    def _():
        back_over.wait_recv()

    loads[5].wait()
    loads[6].wait()
    hist_rows = jnp.dot(
        _gate(_normalise(hist_done[:ROWS, :].astype(jnp.float32)), hist_g[...]), w_ref[...], preferred_element_type=jnp.float32
    ) + x_ref[0].astype(jnp.float32)
    row = seq * ROWS + lax.broadcasted_iota(jnp.int32, (ROWS, MODEL), 0)
    hist_out[0] = jnp.where(row < limit, hist_rows, 0.0).astype(jnp.bfloat16)

    for copy in r_copies:
        copy.wait_recv()
    picked = jnp.dot(pick[...], returned[...], preferred_element_type=jnp.float32)
    cand_out[0, 0] = jnp.dot(
        _gate(_normalise(picked), cand_g[...]), w_ref[...], preferred_element_type=jnp.float32
    ).astype(jnp.bfloat16)

    for copy in to_far:
        copy.wait_send()

    @pl.when(jnp.logical_not(native))
    def _():
        for copy in to_near:
            copy.wait_send()
        q_over.wait_send()

    @pl.when(native)
    def _():
        back_over.wait_send()

    for copy in kv_copies + list(q_copies.values()) + r_copies:
        copy.wait_send()


def local(hist_qu, hist_kv, hist_x, lengths, cand_qu, cand_owner, w_out):
    vmem = pl.BlockSpec(memory_space=pltpu.VMEM)
    hbm = pl.BlockSpec(memory_space=pltpu.HBM)
    arguments = (hist_qu, hist_kv, hist_x, lengths, cand_qu, cand_owner, w_out)
    bf16 = jnp.bfloat16
    return pl.pallas_call(
        kernel,
        out_shape=(
            jax.ShapeDtypeStruct((1, ROWS, MODEL), bf16),
            jax.ShapeDtypeStruct((1, 1, CROWS, MODEL), bf16),
        ),
        in_specs=[hbm] * len(arguments),
        out_specs=(vmem, vmem),
        scratch_shapes=[
            (pltpu.SMEM if a.dtype == jnp.int32 else pltpu.VMEM)(a.shape, a.dtype)
            for a in arguments
        ]
        + [
            pltpu.VMEM((HEADS, 2, ROWS, HEAD_DIM), bf16),
            pltpu.VMEM((HEADS, 2, LENGTH, HEAD_DIM), bf16),
            pltpu.VMEM((2 * ROWS, WIDTH), bf16),
            pltpu.VMEM((2 * ROWS, WIDTH), bf16),
            pltpu.VMEM((2 * CROWS, WIDTH), bf16),
            pltpu.VMEM((CROWS, WIDTH), bf16),
            pltpu.VMEM((ROWS, WIDTH), bf16),
            pltpu.VMEM((PACKED, WIDTH), bf16),
            pltpu.VMEM((PACKED, WIDTH), bf16),
            pltpu.VMEM((PACKED, WIDTH), bf16),
            pltpu.VMEM((PACKED, WIDTH), bf16),
            pltpu.VMEM((CROWS, PACKED), bf16),
            pltpu.SemaphoreType.DMA((len(arguments),)),
            pltpu.SemaphoreType.DMA((64,)),
            pltpu.SemaphoreType.DMA((16, HEADS)),
            pltpu.SemaphoreType.DMA((MESSAGES, HEADS)),
            pltpu.SemaphoreType.DMA((MESSAGES, HEADS)),
            pltpu.SemaphoreType.DMA((MESSAGES, HEADS)),
            pltpu.SemaphoreType.DMA((MESSAGES, HEADS)),
            pltpu.SemaphoreType.DMA((2,)),
            pltpu.SemaphoreType.DMA((2,)),
        ],
        compiler_params=pltpu.CompilerParams(
            collective_id=0, has_side_effects=True, vmem_limit_bytes=63 * 2**20
        ),
    )(*arguments)


def solution(mesh):
    placed = (
        P("users", "seq", None, None),
        P("users", "seq", None, None),
        P("users", "seq", None),
        P("users"),
        P("users", "seq", None, None, None),
        P("users", "seq", None),
        P(),
    )
    return jax.shard_map(
        local,
        mesh=mesh,
        in_specs=placed,
        out_specs=(P("users", "seq", None), P("users", "seq", None, None)),
        check_vma=False,
    )
```

```python
import functools
import math

import jax
import jax.numpy as jnp
from jax import lax
from jax.experimental import pallas as pl
from jax.experimental.pallas import tpu as pltpu
from jax.sharding import PartitionSpec as P

HEADS = 4
HEAD_DIM = 128
WIDTH = HEADS * HEAD_DIM
CAP = 2
TILE = 32
TILES = 12
CROWS = TILES * TILE
ROWS = 128
LENGTH = 2048
MODEL = 1024
EPS = 1e-05
HALF_SCALE = 0.5 / math.sqrt(HEAD_DIM)

ZS, YS = 8, 4
STEPS = 4
MESSAGES = STEPS * 4
Q_ORDER = (12, 13, 14, 15, 4, 8, 5, 9, 6, 10, 7, 11, 1, 2, 3)
PACK = CAP * TILE
PACKED = MESSAGES * PACK
GROUPS = ((0, 8), (8, 8))
AHEAD = 2
QUERY_HEADS = 1
BACK_HEADS = 1


def _mod(value, size):
    return lax.rem(value + 2 * size, size)


def _user(x_hi, z):
    return _mod(x_hi, 2) * ZS + _mod(z, ZS)


def _seq(x_lo, y, core):
    return _mod(x_lo, 2) * (YS * 2) + _mod(y, YS) * 2 + _mod(core, 2)


def _send(src, dst, send_sem, recv_sem, device):
    return pltpu.make_async_remote_copy(
        src_ref=src,
        dst_ref=dst,
        send_sem=send_sem,
        recv_sem=recv_sem,
        device_id=device,
        device_id_type=pl.DeviceIdType.MESH,
    )


def _silu_weights(scores):
    half = scores * HALF_SCALE
    return half + half * jnp.tanh(half)


def _normalise(summed):
    mean = jnp.mean(summed, axis=-1, keepdims=True)
    centred = summed - mean
    spread = jnp.mean(centred * centred, axis=-1, keepdims=True)
    return (centred * lax.rsqrt(spread + EPS)).astype(jnp.bfloat16)


def _every_second(rows, first):
    count = rows.shape[0] // 2
    at = 2 * lax.broadcasted_iota(jnp.int32, (count, 2 * count), 0) + first
    column = lax.broadcasted_iota(jnp.int32, (count, 2 * count), 1)
    return jnp.dot(
        jnp.where(column == at, 1.0, 0.0).astype(jnp.bfloat16),
        rows,
        preferred_element_type=jnp.float32,
    ).astype(jnp.bfloat16)


def _gate(normed, gates):
    return (normed.astype(jnp.float32) * gates.astype(jnp.float32)).astype(jnp.bfloat16)


def kernel(
    qu_hbm, kv_hbm, x_hbm, lengths_hbm, cand_hbm, owner_hbm, w_hbm,
    hist_out, cand_out,
    qu_ref, kv_ref, x_ref, lengths_ref, cand_ref, owner_ref, w_ref,
    own_kv, kv, hist_q, hist_done, cand_rows, cand_g, hist_g, outgoing, arrived, computed,
    returned, pick,
    loaded, kv_send, kv_recv, q_send, q_recv, r_send, r_recv, h_send, h_recv,
):
    user = lax.axis_index("users")
    seq = lax.axis_index("seq")
    x_hi, z = user // ZS, user % ZS
    x_lo, y, core = seq // (YS * 2), (seq // 2) % YS, seq % 2
    home_x = z % 2
    native = x_lo == home_x
    up = 1 - 2 * home_x
    steps = (0, 1, -1, 2)

    def peer(m, back):
        step, a, b = steps[m // 4], (m // 2) % 2, m % 2
        along = -2 if back and step == 2 else step
        return (_user(x_hi + a, z + up * along), _seq(x_lo + b, y, core))

    partner = (user, _seq(x_lo, y, core + 1))
    y_up = (user, _seq(x_lo, y + 1, core))
    y_down = (user, _seq(x_lo, y - 1, core))
    x_other = (user, _seq(x_lo + 1, y, core))
    mate = _user(x_hi, z + 3 * up)

    barrier = pltpu.get_barrier_semaphore()
    greeted = [partner, y_up, y_down]
    greeted += [(mate, _seq(x_lo, y, core)), (mate, _seq(x_lo + 1, y, core))]
    greeted += [peer(m, False) for m in range(1, MESSAGES)]
    greeted += [peer(m, True) for m in range(12, 16)]
    for device in greeted:
        pl.semaphore_signal(
            barrier, inc=1, device_id=device, device_id_type=pl.DeviceIdType.MESH
        )

    pairs = (
        (kv_hbm, kv_ref), (lengths_hbm, lengths_ref), (qu_hbm, qu_ref), (cand_hbm, cand_ref),
        (owner_hbm, owner_ref), (w_hbm, w_ref), (x_hbm, x_ref),
    )
    loads = [pltpu.make_async_copy(a, b, loaded.at[i]) for i, (a, b) in enumerate(pairs)]
    for load in loads:
        load.start()

    loads[0].wait()
    loads[1].wait()
    limit = lengths_ref[0]
    position = seq * ROWS + lax.broadcasted_iota(jnp.int32, (ROWS, WIDTH), 0)
    rows_kv = kv_ref[0].reshape(2 * ROWS, WIDTH)
    keys = _every_second(rows_kv, 0)
    values = jnp.where(position < limit, _every_second(rows_kv, 1), jnp.zeros((), jnp.bfloat16))
    for h in range(HEADS):
        part = slice(h * HEAD_DIM, (h + 1) * HEAD_DIM)
        own_kv[h, 0] = keys[:, part]
        own_kv[h, 1] = values[:, part]
    loads[2].wait()
    hist_q[:ROWS, :] = _every_second(qu_ref[0].reshape(2 * ROWS, WIDTH), 0)

    pl.semaphore_wait(barrier, len(greeted))

    def shard(h, index):
        return kv.at[h, :, pl.ds(pl.multiple_of(index * ROWS, ROWS), ROWS), :]

    home = _seq(home_x, y, core)
    to_far = [
        _send(
            own_kv.at[h], shard(h, seq), kv_send.at[h], kv_recv.at[seq, h], (mate, home)
        )
        for h in range(HEADS)
    ]
    to_near = [
        _send(own_kv.at[h], shard(h, seq), kv_send.at[4 + h], kv_recv.at[seq, h], x_other)
        for h in range(HEADS)
    ]
    q_over = _send(
        hist_q.at[pl.ds(0, ROWS)], hist_q.at[pl.ds(ROWS, ROWS)], h_send.at[0], h_recv.at[0], x_other
    )
    def own_shard(h):
        if h >= 2:
            to_far[h - 2].wait_send()
        to_far[h].start()

        @pl.when(jnp.logical_not(native))
        def _():
            if h >= 2:
                to_near[h - 2].wait_send()
            to_near[h].start()

    own_shard(0)
    own_shard(1)

    @pl.when(native)
    def _():
        kv[:, :, pl.ds(pl.multiple_of(seq * ROWS, ROWS), ROWS), :] = own_kv[...]

    loads[3].wait()
    loads[4].wait()
    owners = [owner_ref[0, 0, t] for t in range(TILES)]

    def slot_rows(index):
        tile = index // TILE
        owner = jnp.zeros_like(index)
        for t in range(TILES):
            owner = jnp.where(tile == t, owners[t], owner)
        again = jnp.zeros_like(index)
        for t in range(TILES - 1):
            again = jnp.where((tile > t) & (owner == owners[t]), 1, again)
        owner_x, owner_z = owner >> 3, owner & 7
        a, b = (owner_x + x_hi) & 1, (owner_z + x_lo) & 1
        apart = (up * (owner_z - z)) & 7
        step = jnp.zeros_like(index)
        for there in ((1, 6), (4, 7), (2, 5)):
            here = (apart == there[0]) | (apart == there[1])
            step = jnp.where(here, 1 + ((1, 6), (4, 7), (2, 5)).index(there), step)
        message = step * 4 + a * 2 + b
        return message * PACK + again * TILE + (index & (TILE - 1))

    for t in range(TILES * TILE // ROWS):
        cand_rows[pl.ds(t * 2 * ROWS, 2 * ROWS), :] = cand_ref[
            0, 0, t * ROWS : (t + 1) * ROWS
        ].reshape(2 * ROWS, WIDTH)
    column = lax.broadcasted_iota(jnp.int32, (8, 2 * CROWS), 1)
    slot = jnp.where((column & 1) == 0, slot_rows(column >> 1), -1)[:1]
    for step in range(STEPS):
        block = pl.ds(step * 4 * PACK, 4 * PACK)
        row = step * 4 * PACK + lax.broadcasted_iota(jnp.int32, (4 * PACK, 2 * CROWS), 0)
        outgoing[block, :] = jnp.dot(
            jnp.where(row == slot, 1.0, 0.0).astype(jnp.bfloat16),
            cand_rows[...],
            preferred_element_type=jnp.float32,
        ).astype(jnp.bfloat16)
    own_rows = pl.ds(0, PACK)
    arrived[own_rows, :] = outgoing[own_rows, :]

    def columns(first, count):
        return pl.ds(first * HEAD_DIM, count * HEAD_DIM)

    q_copies = {}

    def send_queries(h):
        for m in Q_ORDER:
            part = (pl.ds(m * PACK, PACK), columns(h, QUERY_HEADS))
            q_copies[m, h] = _send(
                outgoing.at[part], arrived.at[part], q_send.at[m, h], q_recv.at[m, h], peer(m, False)
            )
            q_copies[m, h].start()

    kv_copies, kv_settled = [], []

    def forward(h, index, device):
        copy = _send(
            shard(h, index),
            shard(h, index),
            kv_send.at[8 + len(kv_copies)],
            kv_recv.at[index, h],
            device,
        )
        copy.start()
        kv_copies.append(copy)
        return copy

    def await_shard(h, index):
        _send(
            shard(h, index), shard(h, index), kv_send.at[0], kv_recv.at[index, h], partner
        ).wait_recv()

    entries = []

    def enter(h):
        if h >= AHEAD:
            for copy in entries[h - AHEAD]:
                copy.wait_send()
                kv_settled.append(copy)
        entries.append([])
        for side in range(2):
            index = _seq(side, y, core)

            @pl.when(jnp.logical_not(jnp.logical_and(native, x_lo == side)))
            def _():
                await_shard(h, index)

            entries[h].append(forward(h, index, y_up))
            entries[h].append(forward(h, index, y_down))
            forward(h, index, partner)

    def first_hop(h):
        for side, dy, onward in ((0, -1, y_up), (1, 1, y_down), (1, -1, None), (0, 1, None)):
            index = _seq(side, y + dy, core)
            await_shard(h, index)
            if onward is not None:
                forward(h, index, onward)
            forward(h, index, partner)

    def second_hop(h):
        for side in range(2):
            index = _seq(side, y + 2, core)
            await_shard(h, index)
            forward(h, index, partner)

    def other_core(h):
        for side in range(2):
            for dy in range(YS):
                await_shard(h, _seq(side, y + dy, core + 1))

    def attend(h, queries, allowed=None):
        scores = lax.dot_general(
            queries, kv[h, 0], (((1,), (1,)), ((), ())), preferred_element_type=jnp.float32
        )
        weights = _silu_weights(scores)
        if allowed is not None:
            weights = jnp.where(allowed, weights, 0.0)
        return jnp.dot(
            weights.astype(jnp.bfloat16), kv[h, 1], preferred_element_type=jnp.float32
        )

    def prepare():
        for t in range(TILES * TILE // ROWS):
            cand_g[pl.ds(t * ROWS, ROWS), :] = _every_second(
                cand_rows[pl.ds(t * 2 * ROWS, 2 * ROWS), :], 1
            )
        hist_g[...] = _every_second(qu_ref[0].reshape(2 * ROWS, WIDTH), 1)
        for t in range(TILES * TILE // ROWS):
            held = slot_rows(t * ROWS + lax.broadcasted_iota(jnp.int32, (ROWS, 128), 0))
            at = lax.broadcasted_iota(jnp.int32, (ROWS, PACKED), 1)
            pick[pl.ds(t * ROWS, ROWS), :] = jnp.where(at == held[:, :1], 1.0, 0.0).astype(jnp.bfloat16)

    r_copies = []

    def group(h, g):
        first, count = GROUPS[g]
        if h % QUERY_HEADS == 0:
            for m in range(max(first, 1), first + count):
                q_copies[m, h].wait_recv()
        rows = pl.ds(first * PACK, count * PACK)
        part = columns(h, 1)
        computed[rows, part] = attend(h, arrived[rows, part]).astype(jnp.bfloat16)
        if (h + 1) % BACK_HEADS:
            return
        start = h + 1 - BACK_HEADS
        for m in range(first, first + count):
            part = (pl.ds(m * PACK, PACK), columns(start, BACK_HEADS))
            if m:
                copy = _send(
                    computed.at[part],
                    returned.at[part],
                    r_send.at[m, start],
                    r_recv.at[m, start],
                    peer(m, True),
                )
                copy.start()
                r_copies.append(copy)
            else:
                returned[part] = computed[part]

    own_shard(2)
    enter(0)
    own_shard(3)
    send_queries(0)

    @pl.when(jnp.logical_not(native))
    def _():
        q_over.start()

    enter(1)
    first_hop(0)
    enter(2)
    send_queries(1)
    first_hop(1)
    second_hop(0)
    enter(3)
    send_queries(2)
    send_queries(3)
    prepare()
    other_core(0)
    first_hop(2)
    second_hop(1)
    group(0, 0)
    first_hop(3)
    second_hop(2)
    group(0, 1)
    other_core(1)
    group(1, 0)
    second_hop(3)
    group(1, 1)
    other_core(2)
    group(2, 0)
    group(2, 1)
    other_core(3)
    group(3, 0)
    group(3, 1)

    back_over = _send(
        hist_done.at[pl.ds(ROWS, ROWS)],
        hist_done.at[pl.ds(0, ROWS)],
        h_send.at[1],
        h_recv.at[1],
        x_other,
    )

    @pl.when(native)
    def _():
        q_over.wait_recv()
        other = _seq(x_lo + 1, y, core)
        key_at = lax.broadcasted_iota(jnp.int32, (2 * ROWS, LENGTH), 1)
        row_at = lax.broadcasted_iota(jnp.int32, (2 * ROWS, LENGTH), 0)
        row_at = row_at + jnp.where(row_at < ROWS, seq * ROWS, (other - 1) * ROWS)
        for h in range(HEADS):
            part = slice(h * HEAD_DIM, (h + 1) * HEAD_DIM)
            hist_done[:, part] = attend(h, hist_q[:, part], key_at <= row_at).astype(jnp.bfloat16)
        back_over.start()

    @pl.when(jnp.logical_not(native))
    def _():
        back_over.wait_recv()

    loads[5].wait()
    loads[6].wait()
    hist_rows = jnp.dot(
        _gate(_normalise(hist_done[:ROWS, :].astype(jnp.float32)), hist_g[...]), w_ref[...], preferred_element_type=jnp.float32
    ) + x_ref[0].astype(jnp.float32)
    row = seq * ROWS + lax.broadcasted_iota(jnp.int32, (ROWS, MODEL), 0)
    hist_out[0] = jnp.where(row < limit, hist_rows, 0.0).astype(jnp.bfloat16)

    for copy in r_copies:
        copy.wait_recv()
    picked = jnp.dot(pick[...], returned[...], preferred_element_type=jnp.float32)
    cand_out[0, 0] = jnp.dot(
        _gate(_normalise(picked), cand_g[...]), w_ref[...], preferred_element_type=jnp.float32
    ).astype(jnp.bfloat16)

    for h in (2, 3):
        to_far[h].wait_send()

    @pl.when(jnp.logical_not(native))
    def _():
        for h in (2, 3):
            to_near[h].wait_send()
        q_over.wait_send()

    @pl.when(native)
    def _():
        back_over.wait_send()

    for copy in kv_copies + list(q_copies.values()) + r_copies:
        if not any(copy is done for done in kv_settled):
            copy.wait_send()


def local(hist_qu, hist_kv, hist_x, lengths, cand_qu, cand_owner, w_out):
    vmem = pl.BlockSpec(memory_space=pltpu.VMEM)
    hbm = pl.BlockSpec(memory_space=pltpu.HBM)
    arguments = (hist_qu, hist_kv, hist_x, lengths, cand_qu, cand_owner, w_out)
    bf16 = jnp.bfloat16
    return pl.pallas_call(
        kernel,
        out_shape=(
            jax.ShapeDtypeStruct((1, ROWS, MODEL), bf16),
            jax.ShapeDtypeStruct((1, 1, CROWS, MODEL), bf16),
        ),
        in_specs=[hbm] * len(arguments),
        out_specs=(vmem, vmem),
        scratch_shapes=[
            (pltpu.SMEM if a.dtype == jnp.int32 else pltpu.VMEM)(a.shape, a.dtype)
            for a in arguments
        ]
        + [
            pltpu.VMEM((HEADS, 2, ROWS, HEAD_DIM), bf16),
            pltpu.VMEM((HEADS, 2, LENGTH, HEAD_DIM), bf16),
            pltpu.VMEM((2 * ROWS, WIDTH), bf16),
            pltpu.VMEM((2 * ROWS, WIDTH), bf16),
            pltpu.VMEM((2 * CROWS, WIDTH), bf16),
            pltpu.VMEM((CROWS, WIDTH), bf16),
            pltpu.VMEM((ROWS, WIDTH), bf16),
            pltpu.VMEM((PACKED, WIDTH), bf16),
            pltpu.VMEM((PACKED, WIDTH), bf16),
            pltpu.VMEM((PACKED, WIDTH), bf16),
            pltpu.VMEM((PACKED, WIDTH), bf16),
            pltpu.VMEM((CROWS, PACKED), bf16),
            pltpu.SemaphoreType.DMA((len(arguments),)),
            pltpu.SemaphoreType.DMA((64,)),
            pltpu.SemaphoreType.DMA((16, HEADS)),
            pltpu.SemaphoreType.DMA((MESSAGES, HEADS)),
            pltpu.SemaphoreType.DMA((MESSAGES, HEADS)),
            pltpu.SemaphoreType.DMA((MESSAGES, HEADS)),
            pltpu.SemaphoreType.DMA((MESSAGES, HEADS)),
            pltpu.SemaphoreType.DMA((2,)),
            pltpu.SemaphoreType.DMA((2,)),
        ],
        compiler_params=pltpu.CompilerParams(
            collective_id=0, has_side_effects=True, vmem_limit_bytes=63 * 2**20
        ),
    )(*arguments)


def solution(mesh):
    placed = (
        P("users", "seq", None, None),
        P("users", "seq", None, None),
        P("users", "seq", None),
        P("users"),
        P("users", "seq", None, None, None),
        P("users", "seq", None),
        P(),
    )
    return jax.shard_map(
        local,
        mesh=mesh,
        in_specs=placed,
        out_specs=(P("users", "seq", None), P("users", "seq", None, None)),
        check_vma=False,
    )
```

```python
import functools
import math

import jax
import jax.numpy as jnp
from jax import lax
from jax.experimental import pallas as pl
from jax.experimental.pallas import tpu as pltpu
from jax.sharding import PartitionSpec as P

HEADS = 4
HEAD_DIM = 128
WIDTH = HEADS * HEAD_DIM
CAP = 2
TILE = 32
TILES = 12
CROWS = TILES * TILE
ROWS = 128
LENGTH = 2048
MODEL = 1024
EPS = 1e-05
HALF_SCALE = 0.5 / math.sqrt(HEAD_DIM)

ZS, YS = 8, 4
STEPS = 4
MESSAGES = STEPS * 4
Q_ORDER = (12, 13, 14, 15, 4, 8, 5, 9, 6, 10, 7, 11, 1, 2, 3)
PACK = CAP * TILE
PACKED = MESSAGES * PACK
GROUPS = ((0, 8), (8, 8))
AHEAD = 4
QUERY_HEADS = 1
BACK_HEADS = 1


def _mod(value, size):
    return lax.rem(value + 2 * size, size)


def _user(x_hi, z):
    return _mod(x_hi, 2) * ZS + _mod(z, ZS)


def _seq(x_lo, y, core):
    return _mod(x_lo, 2) * (YS * 2) + _mod(y, YS) * 2 + _mod(core, 2)


def _send(src, dst, send_sem, recv_sem, device):
    return pltpu.make_async_remote_copy(
        src_ref=src,
        dst_ref=dst,
        send_sem=send_sem,
        recv_sem=recv_sem,
        device_id=device,
        device_id_type=pl.DeviceIdType.MESH,
    )


def _silu_weights(scores):
    half = scores * HALF_SCALE
    return half + half * jnp.tanh(half)


def _normalise(summed):
    mean = jnp.mean(summed, axis=-1, keepdims=True)
    centred = summed - mean
    spread = jnp.mean(centred * centred, axis=-1, keepdims=True)
    return (centred * lax.rsqrt(spread + EPS)).astype(jnp.bfloat16)


def _every_second(rows, first):
    count = rows.shape[0] // 2
    at = 2 * lax.broadcasted_iota(jnp.int32, (count, 2 * count), 0) + first
    column = lax.broadcasted_iota(jnp.int32, (count, 2 * count), 1)
    return jnp.dot(
        jnp.where(column == at, 1.0, 0.0).astype(jnp.bfloat16),
        rows,
        preferred_element_type=jnp.float32,
    ).astype(jnp.bfloat16)


def _gate(normed, gates):
    return (normed.astype(jnp.float32) * gates.astype(jnp.float32)).astype(jnp.bfloat16)


def kernel(
    qu_hbm, kv_hbm, x_hbm, lengths_hbm, cand_hbm, owner_hbm, w_hbm,
    hist_out, cand_out,
    qu_ref, kv_ref, x_ref, lengths_ref, cand_ref, owner_ref, w_ref,
    own_kv, kv, hist_q, hist_done, cand_rows, cand_g, hist_g, outgoing, arrived, computed,
    returned, pick,
    loaded, kv_send, kv_recv, q_send, q_recv, r_send, r_recv, h_send, h_recv,
):
    user = lax.axis_index("users")
    seq = lax.axis_index("seq")
    x_hi, z = user // ZS, user % ZS
    x_lo, y, core = seq // (YS * 2), (seq // 2) % YS, seq % 2
    home_x = z % 2
    native = x_lo == home_x
    up = 1 - 2 * home_x
    steps = (0, 1, -1, 2)

    def peer(m, back):
        step, a, b = steps[m // 4], (m // 2) % 2, m % 2
        along = -2 if back and step == 2 else step
        return (_user(x_hi + a, z + up * along), _seq(x_lo + b, y, core))

    partner = (user, _seq(x_lo, y, core + 1))
    y_up = (user, _seq(x_lo, y + 1, core))
    y_down = (user, _seq(x_lo, y - 1, core))
    x_other = (user, _seq(x_lo + 1, y, core))
    mate = _user(x_hi, z + 3 * up)

    barrier = pltpu.get_barrier_semaphore()
    greeted = [partner, y_up, y_down]
    greeted += [(mate, _seq(x_lo, y, core)), (mate, _seq(x_lo + 1, y, core))]
    greeted += [peer(m, False) for m in range(1, MESSAGES)]
    greeted += [peer(m, True) for m in range(12, 16)]
    for device in greeted:
        pl.semaphore_signal(
            barrier, inc=1, device_id=device, device_id_type=pl.DeviceIdType.MESH
        )

    pairs = (
        (kv_hbm, kv_ref), (lengths_hbm, lengths_ref), (qu_hbm, qu_ref), (cand_hbm, cand_ref),
        (owner_hbm, owner_ref), (w_hbm, w_ref), (x_hbm, x_ref),
    )
    loads = [pltpu.make_async_copy(a, b, loaded.at[i]) for i, (a, b) in enumerate(pairs)]
    for load in loads:
        load.start()

    loads[0].wait()
    loads[1].wait()
    limit = lengths_ref[0]
    position = seq * ROWS + lax.broadcasted_iota(jnp.int32, (ROWS, WIDTH), 0)
    rows_kv = kv_ref[0].reshape(2 * ROWS, WIDTH)
    keys = _every_second(rows_kv, 0)
    values = jnp.where(position < limit, _every_second(rows_kv, 1), jnp.zeros((), jnp.bfloat16))
    for h in range(HEADS):
        part = slice(h * HEAD_DIM, (h + 1) * HEAD_DIM)
        own_kv[h, 0] = keys[:, part]
        own_kv[h, 1] = values[:, part]
    loads[2].wait()
    hist_q[:ROWS, :] = _every_second(qu_ref[0].reshape(2 * ROWS, WIDTH), 0)

    pl.semaphore_wait(barrier, len(greeted))

    def shard(h, index):
        return kv.at[h, :, pl.ds(pl.multiple_of(index * ROWS, ROWS), ROWS), :]

    home = _seq(home_x, y, core)
    to_far = [
        _send(
            own_kv.at[h], shard(h, seq), kv_send.at[h], kv_recv.at[seq, h], (mate, home)
        )
        for h in range(HEADS)
    ]
    to_near = [
        _send(own_kv.at[h], shard(h, seq), kv_send.at[4 + h], kv_recv.at[seq, h], x_other)
        for h in range(HEADS)
    ]
    q_over = _send(
        hist_q.at[pl.ds(0, ROWS)], hist_q.at[pl.ds(ROWS, ROWS)], h_send.at[0], h_recv.at[0], x_other
    )
    def own_shard(h):
        if h >= 2:
            to_far[h - 2].wait_send()
        to_far[h].start()

        @pl.when(jnp.logical_not(native))
        def _():
            if h >= 2:
                to_near[h - 2].wait_send()
            to_near[h].start()

    own_shard(0)
    own_shard(1)

    @pl.when(native)
    def _():
        kv[:, :, pl.ds(pl.multiple_of(seq * ROWS, ROWS), ROWS), :] = own_kv[...]

    loads[3].wait()
    loads[4].wait()
    owners = [owner_ref[0, 0, t] for t in range(TILES)]

    def slot_rows(index):
        tile = index // TILE
        owner = jnp.zeros_like(index)
        for t in range(TILES):
            owner = jnp.where(tile == t, owners[t], owner)
        again = jnp.zeros_like(index)
        for t in range(TILES - 1):
            again = jnp.where((tile > t) & (owner == owners[t]), 1, again)
        owner_x, owner_z = owner >> 3, owner & 7
        a, b = (owner_x + x_hi) & 1, (owner_z + x_lo) & 1
        apart = (up * (owner_z - z)) & 7
        step = jnp.zeros_like(index)
        for there in ((1, 6), (4, 7), (2, 5)):
            here = (apart == there[0]) | (apart == there[1])
            step = jnp.where(here, 1 + ((1, 6), (4, 7), (2, 5)).index(there), step)
        message = step * 4 + a * 2 + b
        return message * PACK + again * TILE + (index & (TILE - 1))

    for t in range(TILES * TILE // ROWS):
        cand_rows[pl.ds(t * 2 * ROWS, 2 * ROWS), :] = cand_ref[
            0, 0, t * ROWS : (t + 1) * ROWS
        ].reshape(2 * ROWS, WIDTH)
    column = lax.broadcasted_iota(jnp.int32, (8, 2 * CROWS), 1)
    slot = jnp.where((column & 1) == 0, slot_rows(column >> 1), -1)[:1]
    for step in range(STEPS):
        block = pl.ds(step * 4 * PACK, 4 * PACK)
        row = step * 4 * PACK + lax.broadcasted_iota(jnp.int32, (4 * PACK, 2 * CROWS), 0)
        outgoing[block, :] = jnp.dot(
            jnp.where(row == slot, 1.0, 0.0).astype(jnp.bfloat16),
            cand_rows[...],
            preferred_element_type=jnp.float32,
        ).astype(jnp.bfloat16)
    own_rows = pl.ds(0, PACK)
    arrived[own_rows, :] = outgoing[own_rows, :]

    def columns(first, count):
        return pl.ds(first * HEAD_DIM, count * HEAD_DIM)

    q_copies = {}

    def send_queries(h):
        for m in Q_ORDER:
            part = (pl.ds(m * PACK, PACK), columns(h, QUERY_HEADS))
            q_copies[m, h] = _send(
                outgoing.at[part], arrived.at[part], q_send.at[m, h], q_recv.at[m, h], peer(m, False)
            )
            q_copies[m, h].start()

    kv_copies, kv_settled = [], []

    def forward(h, index, device):
        copy = _send(
            shard(h, index),
            shard(h, index),
            kv_send.at[8 + len(kv_copies)],
            kv_recv.at[index, h],
            device,
        )
        copy.start()
        kv_copies.append(copy)
        return copy

    def await_shard(h, index):
        _send(
            shard(h, index), shard(h, index), kv_send.at[0], kv_recv.at[index, h], partner
        ).wait_recv()

    entries = []

    def enter(h):
        if h >= AHEAD:
            for copy in entries[h - AHEAD]:
                copy.wait_send()
                kv_settled.append(copy)
        entries.append([])
        for side in range(2):
            index = _seq(side, y, core)

            @pl.when(jnp.logical_not(jnp.logical_and(native, x_lo == side)))
            def _():
                await_shard(h, index)

            entries[h].append(forward(h, index, y_up))
            entries[h].append(forward(h, index, y_down))
            forward(h, index, partner)

    def first_hop(h):
        for side, dy, onward in ((0, -1, y_up), (1, 1, y_down), (1, -1, None), (0, 1, None)):
            index = _seq(side, y + dy, core)
            await_shard(h, index)
            if onward is not None:
                forward(h, index, onward)
            forward(h, index, partner)

    def second_hop(h):
        for side in range(2):
            index = _seq(side, y + 2, core)
            await_shard(h, index)
            forward(h, index, partner)

    def other_core(h):
        for side in range(2):
            for dy in range(YS):
                await_shard(h, _seq(side, y + dy, core + 1))

    def attend(h, queries, allowed=None):
        scores = lax.dot_general(
            queries, kv[h, 0], (((1,), (1,)), ((), ())), preferred_element_type=jnp.float32
        )
        weights = _silu_weights(scores)
        if allowed is not None:
            weights = jnp.where(allowed, weights, 0.0)
        return jnp.dot(
            weights.astype(jnp.bfloat16), kv[h, 1], preferred_element_type=jnp.float32
        )

    def prepare():
        for t in range(TILES * TILE // ROWS):
            cand_g[pl.ds(t * ROWS, ROWS), :] = _every_second(
                cand_rows[pl.ds(t * 2 * ROWS, 2 * ROWS), :], 1
            )
        hist_g[...] = _every_second(qu_ref[0].reshape(2 * ROWS, WIDTH), 1)
        for t in range(TILES * TILE // ROWS):
            held = slot_rows(t * ROWS + lax.broadcasted_iota(jnp.int32, (ROWS, 128), 0))
            at = lax.broadcasted_iota(jnp.int32, (ROWS, PACKED), 1)
            pick[pl.ds(t * ROWS, ROWS), :] = jnp.where(at == held[:, :1], 1.0, 0.0).astype(jnp.bfloat16)

    r_copies = []

    def group(h, g):
        first, count = GROUPS[g]
        if h % QUERY_HEADS == 0:
            for m in range(max(first, 1), first + count):
                q_copies[m, h].wait_recv()
        rows = pl.ds(first * PACK, count * PACK)
        part = columns(h, 1)
        computed[rows, part] = attend(h, arrived[rows, part]).astype(jnp.bfloat16)
        if (h + 1) % BACK_HEADS:
            return
        start = h + 1 - BACK_HEADS
        for m in reversed(range(first, first + count)):
            part = (pl.ds(m * PACK, PACK), columns(start, BACK_HEADS))
            if m:
                copy = _send(
                    computed.at[part],
                    returned.at[part],
                    r_send.at[m, start],
                    r_recv.at[m, start],
                    peer(m, True),
                )
                copy.start()
                r_copies.append(copy)
            else:
                returned[part] = computed[part]

    own_shard(2)
    send_queries(0)
    enter(0)
    own_shard(3)
    send_queries(1)
    @pl.when(jnp.logical_not(native))
    def _():
        q_over.start()
    enter(1)
    first_hop(0)
    send_queries(2)
    enter(2)
    send_queries(3)
    first_hop(1)
    second_hop(0)
    enter(3)
    prepare()
    other_core(0)
    first_hop(2)
    group(0, 0)
    second_hop(1)
    first_hop(3)
    group(0, 1)
    second_hop(2)
    other_core(1)
    group(1, 0)
    second_hop(3)
    group(1, 1)
    other_core(2)
    group(2, 0)
    group(2, 1)
    other_core(3)
    group(3, 1)
    group(3, 0)

    back_over = _send(
        hist_done.at[pl.ds(ROWS, ROWS)],
        hist_done.at[pl.ds(0, ROWS)],
        h_send.at[1],
        h_recv.at[1],
        x_other,
    )

    @pl.when(native)
    def _():
        q_over.wait_recv()
        other = _seq(x_lo + 1, y, core)
        key_at = lax.broadcasted_iota(jnp.int32, (2 * ROWS, LENGTH), 1)
        row_at = lax.broadcasted_iota(jnp.int32, (2 * ROWS, LENGTH), 0)
        row_at = row_at + jnp.where(row_at < ROWS, seq * ROWS, (other - 1) * ROWS)
        for h in range(HEADS):
            part = slice(h * HEAD_DIM, (h + 1) * HEAD_DIM)
            hist_done[:, part] = attend(h, hist_q[:, part], key_at <= row_at).astype(jnp.bfloat16)
        back_over.start()

    @pl.when(jnp.logical_not(native))
    def _():
        back_over.wait_recv()

    loads[5].wait()
    loads[6].wait()
    hist_rows = jnp.dot(
        _gate(_normalise(hist_done[:ROWS, :].astype(jnp.float32)), hist_g[...]), w_ref[...], preferred_element_type=jnp.float32
    ) + x_ref[0].astype(jnp.float32)
    row = seq * ROWS + lax.broadcasted_iota(jnp.int32, (ROWS, MODEL), 0)
    hist_out[0] = jnp.where(row < limit, hist_rows, 0.0).astype(jnp.bfloat16)

    for copy in r_copies:
        copy.wait_recv()
    picked = jnp.dot(pick[...], returned[...], preferred_element_type=jnp.float32)
    cand_out[0, 0] = jnp.dot(
        _gate(_normalise(picked), cand_g[...]), w_ref[...], preferred_element_type=jnp.float32
    ).astype(jnp.bfloat16)

    for h in (2, 3):
        to_far[h].wait_send()

    @pl.when(jnp.logical_not(native))
    def _():
        for h in (2, 3):
            to_near[h].wait_send()
        q_over.wait_send()

    @pl.when(native)
    def _():
        back_over.wait_send()

    for copy in kv_copies + list(q_copies.values()) + r_copies:
        if not any(copy is done for done in kv_settled):
            copy.wait_send()


def local(hist_qu, hist_kv, hist_x, lengths, cand_qu, cand_owner, w_out):
    vmem = pl.BlockSpec(memory_space=pltpu.VMEM)
    hbm = pl.BlockSpec(memory_space=pltpu.HBM)
    arguments = (hist_qu, hist_kv, hist_x, lengths, cand_qu, cand_owner, w_out)
    bf16 = jnp.bfloat16
    return pl.pallas_call(
        kernel,
        out_shape=(
            jax.ShapeDtypeStruct((1, ROWS, MODEL), bf16),
            jax.ShapeDtypeStruct((1, 1, CROWS, MODEL), bf16),
        ),
        in_specs=[hbm] * len(arguments),
        out_specs=(vmem, vmem),
        scratch_shapes=[
            (pltpu.SMEM if a.dtype == jnp.int32 else pltpu.VMEM)(a.shape, a.dtype)
            for a in arguments
        ]
        + [
            pltpu.VMEM((HEADS, 2, ROWS, HEAD_DIM), bf16),
            pltpu.VMEM((HEADS, 2, LENGTH, HEAD_DIM), bf16),
            pltpu.VMEM((2 * ROWS, WIDTH), bf16),
            pltpu.VMEM((2 * ROWS, WIDTH), bf16),
            pltpu.VMEM((2 * CROWS, WIDTH), bf16),
            pltpu.VMEM((CROWS, WIDTH), bf16),
            pltpu.VMEM((ROWS, WIDTH), bf16),
            pltpu.VMEM((PACKED, WIDTH), bf16),
            pltpu.VMEM((PACKED, WIDTH), bf16),
            pltpu.VMEM((PACKED, WIDTH), bf16),
            pltpu.VMEM((PACKED, WIDTH), bf16),
            pltpu.VMEM((CROWS, PACKED), bf16),
            pltpu.SemaphoreType.DMA((len(arguments),)),
            pltpu.SemaphoreType.DMA((64,)),
            pltpu.SemaphoreType.DMA((16, HEADS)),
            pltpu.SemaphoreType.DMA((MESSAGES, HEADS)),
            pltpu.SemaphoreType.DMA((MESSAGES, HEADS)),
            pltpu.SemaphoreType.DMA((MESSAGES, HEADS)),
            pltpu.SemaphoreType.DMA((MESSAGES, HEADS)),
            pltpu.SemaphoreType.DMA((2,)),
            pltpu.SemaphoreType.DMA((2,)),
        ],
        compiler_params=pltpu.CompilerParams(
            collective_id=0, has_side_effects=True, vmem_limit_bytes=63 * 2**20
        ),
    )(*arguments)


def solution(mesh):
    placed = (
        P("users", "seq", None, None),
        P("users", "seq", None, None),
        P("users", "seq", None),
        P("users"),
        P("users", "seq", None, None, None),
        P("users", "seq", None),
        P(),
    )
    return jax.shard_map(
        local,
        mesh=mesh,
        in_specs=placed,
        out_specs=(P("users", "seq", None), P("users", "seq", None, None)),
        check_vma=False,
    )
```
